32 devices in a mesh: rec: 4 (over y, core), tract: 8 (over z, x).
Axes of the slice: x: 2, y: 2, z: 4, core: 2. Of those that a mesh axis runs over, the one named last changes fastest.
Arguments:
- rep_weights: float32 [80, 131072], P(None, ('rec', 'tract')), may hold values from 0.5 to 2
- covariate_codes: int32 [5, 131072], P(None, ('rec', 'tract')), may hold values from 0 to 15
- tract_of: int32 [131072, 1], P(('rec', 'tract')), may hold values from 0 to 7; in each aligned block of 4096 rows (0 to 4095, 4096 to 8191, ...) at most 1536 rows name the same one
- log_income: bfloat16 [131072], P(('rec', 'tract')), may hold values from -5 to 5
- controls: float32 [64], replicated, may hold values from 7782 to 10240
- threshold_grid: int32 [2048], replicated, may hold values from 0 to 4095
Outputs:
- calibrated: float32 [80, 131072], P(None, ('rec', 'tract'))
- income_tables: float32 [8, 80, 2048], P('tract', None, 'rec')
The draws below stay inside these ranges and needn't reach their ends.
Inputs may be any that keep to these rules, and one draw needn't show every extreme that they name: `tract_of`: among the 4096 persons of one device at most 1536 share a tract; in some aligned blocks of 4096 persons one tract has exactly 1536.
All inputs are finite; a program needn't handle non-finite values.
Results may differ from the reference program's by a relative error of at most 0.0003.
Values may be sent and summed in bfloat16 or wider, within the bound.
A program may use at most 128 MiB of HBM per device.

```python
import math
import jax
import jax.numpy as jnp
import numpy as np
from jax import lax

REPS = 80
CTRL = 64
VARS = 5
THRESH = 2048
R_DEV = 4096
TRACTS = 8
CAP = 1536
TOTAL = 131072


odd_factors = [3, 5, 7, 11]


level_shifts = [1, 6, 11, 3]


copy_limits = [13, 11, 9, 12]


def person_codes(key):
    base_key, pick_key, copy_key = jax.random.split(key, 3)
    first = jax.random.randint(base_key, (TOTAL,), 0, 16, dtype=jnp.int32)
    uniform_codes = jax.random.randint(pick_key, (VARS - 1, TOTAL), 0, 16, dtype=jnp.int32)
    copy_draw = jax.random.randint(copy_key, (VARS - 1, TOTAL), 0, 20, dtype=jnp.int32)
    rows = [first]
    for variable in range(1, VARS):
        table_index = (variable - 1) % 4
        mapped = (first * odd_factors[table_index] + level_shifts[table_index]) % 16
        copied = copy_draw[variable - 1] < copy_limits[table_index]
        rows.append(jnp.where(copied, mapped, uniform_codes[variable - 1]))
    return jnp.stack(rows, axis=0).astype(jnp.int32)


def draw_covariate_codes(key, part):
    return person_codes(jax.random.fold_in(key, 11))


def draw_rep_weights(key, part):
    codes = person_codes(jax.random.fold_in(key, 11))
    own_key = jax.random.fold_in(key, 23)
    level_key, cell_key, noise_key = jax.random.split(own_key, 3)
    levels = jnp.exp(jax.random.uniform(level_key, (REPS, 1), jnp.float32, -0.25, 0.25))
    cells = jnp.exp(jax.random.uniform(cell_key, (REPS, 16), jnp.float32, -0.35, 0.35))
    noise = jnp.exp(jax.random.uniform(noise_key, (REPS, TOTAL), jnp.float32, -0.25, 0.25))
    cell_factor = jnp.take(cells, codes[0], axis=1)
    values = jnp.clip(levels * cell_factor * noise, 0.5, 2.0)
    return values.astype(jnp.float32)


def draw_log_income(key, part):
    first_key = jax.random.fold_in(key, 0)
    values = jnp.clip(jax.random.normal(first_key, (TOTAL,), jnp.float32), -5.0, 5.0)
    return values.astype(jnp.bfloat16)


def plant(values, stream_key, least, top_value):
    longest = values.shape.index(max(values.shape))
    spots = []
    for shift in (0, 1):
        where = [jax.random.randint(jax.random.fold_in(stream_key, axis), (), 0, length) for axis, length in enumerate(values.shape)]
        where[longest] = (where[longest] + shift) % values.shape[longest]
        spots.append(tuple(where))
    return values.at[spots[0]].set(least).at[spots[1]].set(top_value)


def deal_out(key, own, number, rows, amount, top, bound, slope):
    ranking = jax.random.permutation(key, amount)
    packed, usual = load_shares(amount, rows * top, bound, slope, True), load_shares(amount, rows * top, bound, slope, False)
    places = jnp.arange(amount)

    def named(tallies, turn):
        used = int((tallies > 0).sum())
        fixed = max(1, used // 4)
        shifted = fixed + (places - fixed + turn * (used - fixed)) % max(1, amount - fixed)
        return jnp.zeros((amount,), jnp.int32).at[ranking[jnp.where(places < fixed, places, shifted)]].set(jnp.asarray(tallies, jnp.int32))

    tallies = jnp.where(number % 4 == 0, named(packed, number // 4), named(usual, number - number // 4 - 1))
    mixed = jax.random.permutation(jax.random.fold_in(own, 3), amount)
    giver, taker = mixed[0:amount // 2 * 2:2], mixed[1:amount // 2 * 2:2]
    room = jnp.minimum(tallies[giver] - 1, bound - tallies[taker]) // 2
    room = jnp.where((giver == ranking[0]) | (taker == ranking[0]) | (tallies[taker] == 0), 0, jnp.maximum(room, 0))
    shifted = jax.random.randint(jax.random.fold_in(own, 4), (amount // 2,), 0, 1 << 20) % (room + 1)
    tallies = tallies.at[giver].add(-shifted).at[taker].add(shifted)
    labels = jnp.searchsorted(jnp.cumsum(tallies), jnp.arange(rows * top), side="right").astype(jnp.int32)
    listing = labels.reshape(top, rows).T
    listing = listing[jax.random.permutation(jax.random.fold_in(own, 1), rows)]
    turn = jax.random.randint(jax.random.fold_in(own, 2), (rows, 1), 0, top)
    return jnp.take_along_axis(listing, (jnp.arange(top)[None, :] + turn) % top, axis=1)


def load_shares(number_of, total, reach, skew, full):
    portions = [(1 << 20) // math.isqrt(rank ** skew) + 1 for rank in range(1, number_of + 1)]
    largest = reach if full else min(reach, max(-(-total // number_of), total * portions[0] // sum(portions)))
    least = 1 if total - largest >= number_of - 1 else 0
    holding, spare = [largest] + [least] * (number_of - 1), total - largest - least * (number_of - 1)
    while spare > 0:
        free = [i for i in range(1, number_of) if holding[i] < largest] or [i for i in range(1, number_of) if holding[i] < reach]
        pool, left = sum([portions[i] for i in free]), spare
        for i in free:
            more = min(reach - holding[i], max(1, left * portions[i] // pool), spare)
            holding[i] = holding[i] + more
            spare = spare - more
    return np.array(holding)


def setup_inputs(seed: int = 0) -> dict:
    splits = jax.random.split(jax.random.key(seed), 7)
    rep_weights = draw_rep_weights(jax.random.fold_in(splits[6], 71), 0)
    covariate_codes = draw_covariate_codes(jax.random.fold_in(splits[6], 71), 0)
    tract_of_keys = jax.random.split(jax.random.fold_in(splits[2], 1), TOTAL // R_DEV)
    tract_of_turns = jax.random.permutation(jax.random.fold_in(splits[2], 3), TOTAL // R_DEV)
    tract_of = jax.vmap(lambda own, number: deal_out(jax.random.fold_in(splits[2], 2), own, number, R_DEV, TRACTS, 1, CAP, 2))(tract_of_keys, tract_of_turns).reshape((TOTAL, 1))
    log_income = draw_log_income(jax.random.fold_in(splits[6], 71), 0)
    controls = jnp.clip(jax.random.uniform(splits[4], (CTRL,), jnp.float32, 7782.0, 10240.0), 7782.0, 10240.0)
    threshold_grid = plant(jax.random.randint(splits[5], (THRESH,), 0, 4096), jax.random.fold_in(splits[5], 1), 0, 4095).astype(jnp.int32)
    return dict(rep_weights=rep_weights, covariate_codes=covariate_codes, tract_of=tract_of, log_income=log_income, controls=controls, threshold_grid=threshold_grid)


smooth_width = 3.0 / 8192.0
grid_middle = 2048.0
grid_step = 3.0 / 2048.0
base_levels = 16
first_kept = 4

def design(covariate_codes):
    level_codes = jnp.arange(base_levels, dtype=jnp.int32)
    kept_levels = jnp.arange(first_kept, base_levels, dtype=jnp.int32)
    groups = [covariate_codes[0][None, :] == level_codes[:, None]]
    for variable in range(1, covariate_codes.shape[0]):
        groups.append(covariate_codes[variable][None, :] == kept_levels[:, None])
    return jnp.concatenate(groups, axis=0).astype(jnp.float32)

def kept_columns(variables):
    columns_list = list(range(base_levels))
    for variable in range(1, variables):
        columns_list += [variable * base_levels + level_code for level_code in range(first_kept, base_levels)]
    return np.array(columns_list, dtype=np.int32)

def solve_controls(gram_sums, totals, controls):
    factor = jnp.linalg.cholesky(gram_sums)
    gap = (controls[None, :] - totals)[:, :, None]
    middle = lax.linalg.triangular_solve(factor, gap, left_side=True, lower=True)
    result = lax.linalg.triangular_solve(factor, middle, left_side=True, lower=True, transpose_a=True)
    return result[:, :, 0]

def reference(rep_weights, covariate_codes, tract_of, log_income, controls, threshold_grid):
    weights_rows = rep_weights.T
    width = VARS * base_levels
    whole_gram = jnp.zeros((width, width, REPS), jnp.float32)
    single_sums = []
    for first_var in range(VARS):
        single_sums.append(jax.ops.segment_sum(weights_rows, covariate_codes[first_var], num_segments=base_levels))
        for second_var in range(VARS):
            joint = covariate_codes[first_var] * base_levels + covariate_codes[second_var]
            joint_sums = jax.ops.segment_sum(weights_rows, joint, num_segments=base_levels * base_levels)
            whole_gram = whole_gram.at[first_var * base_levels:(first_var + 1) * base_levels, second_var * base_levels:(second_var + 1) * base_levels].set(joint_sums.reshape(base_levels, base_levels, REPS))
    chosen = kept_columns(VARS)
    gram_sums = jnp.transpose(whole_gram[chosen][:, chosen], (2, 0, 1))
    totals = jnp.concatenate(single_sums, axis=0)[chosen].T
    multipliers = solve_controls(gram_sums, totals, controls)
    design_rows = design(covariate_codes)
    factors = 1.0 + jnp.dot(multipliers, design_rows, precision=lax.Precision.HIGHEST)
    calibrated = rep_weights * factors
    sent_weights = calibrated.astype(jnp.bfloat16)
    centers = (threshold_grid.astype(jnp.float32) - grid_middle) * grid_step
    tract_ids = tract_of[:, 0]
    sorted_rows = jnp.argsort(tract_ids, stable=True).astype(jnp.int32)
    sorted_weights = jnp.take(sent_weights, sorted_rows, axis=1)
    sorted_income = jnp.take(log_income, sorted_rows).astype(jnp.float32)
    sorted_tracts = jnp.take(tract_ids, sorted_rows)
    block_rows = math.gcd(TOTAL, 4096)
    block_count = TOTAL // block_rows
    weight_blocks = jnp.transpose(sorted_weights.reshape(REPS, block_count, block_rows), (1, 0, 2))
    income_blocks = sorted_income.reshape(block_count, block_rows)
    tract_blocks = sorted_tracts.reshape(block_count, block_rows)

    def block_step(table_sum, block_data):
        weight_block, income_block, tract_block = block_data
        smoothed = jax.nn.sigmoid((centers[None, :] - income_block[:, None]) / smooth_width).astype(jnp.bfloat16)
        smooth_f32 = smoothed.astype(jnp.float32)
        weights_f32 = weight_block.astype(jnp.float32)
        last_tract = tract_block[block_rows - 1]

        def more_tracts(state):
            return state[0] <= last_tract

        def add_tract(state):
            tract_index, running = state
            in_tract = tract_block == tract_index
            addition = jnp.dot(jnp.where(in_tract[None, :], weights_f32, 0.0).astype(jnp.float32), smooth_f32.astype(jnp.float32), preferred_element_type=jnp.float32)
            return (tract_index + 1, running.at[tract_index].add(addition))
        state = lax.while_loop(more_tracts, add_tract, (tract_block[0], table_sum))
        return (state[1], None)
    start_table = jnp.zeros((TRACTS, REPS, THRESH), jnp.float32)
    table_sum, _ = lax.scan(block_step, start_table, (weight_blocks, income_blocks, tract_blocks))
    income_tables = table_sum / float(TOTAL // TRACTS)
    return (calibrated, income_tables)
```

```python
import functools

import jax
import jax.numpy as jnp
from jax import lax
from jax.experimental import pallas as pl
from jax.experimental.pallas import tpu as pltpu
from jax.sharding import PartitionSpec as P

smooth_width = 3.0 / 8192.0
grid_middle = 2048.0
grid_step = 3.0 / 2048.0
base_levels = 16
first_kept = 4
vmem_bytes = 48 * 1024 * 1024
bf16 = jnp.bfloat16
f32 = jnp.float32


def pair_layout(variables):
    offsets, row = {}, 0
    for u in range(variables):
        first = 0 if u == 0 else first_kept
        for v in range(u + 1, variables):
            offsets[u, v] = row
            row += (base_levels - first) * base_levels
    singles = row
    row += variables * base_levels
    return offsets, singles, row


def split3(value, axis):
    high = value.astype(bf16)
    rest = value - high.astype(f32)
    middle = rest.astype(bf16)
    low = (rest - middle.astype(f32)).astype(bf16)
    return jnp.concatenate([high, middle, low], axis=axis)


def one_hot(key, rows):
    width = key.shape[1]
    row = lax.broadcasted_iota(jnp.int32, (rows, width), 0)
    return jnp.where(row == key, 1.0, 0.0).astype(bf16)


def gram_kernel(w_ref, codes_ref, out_ref, pairs, total):
    step = pl.program_id(0)
    variables, _ = codes_ref.shape
    reps = w_ref.shape[0]
    offsets, singles, rows = pair_layout(variables)

    @pl.when(step == 0)
    def _():
        total[...] = jnp.zeros_like(total)

    pieces = split3(w_ref[...], 0)
    for (u, v), row in offsets.items():
        first = 0 if u == 0 else first_kept
        key = (codes_ref[u : u + 1, :] - first) * base_levels + codes_ref[v : v + 1, :]
        count = (base_levels - first) * base_levels
        pairs[row : row + count, :] = one_hot(key, count)
    for v in range(variables):
        row = singles + v * base_levels
        pairs[row : row + base_levels, :] = one_hot(codes_ref[v : v + 1, :], base_levels)
    total[...] += lax.dot_general(
        pairs[...], pieces, (((1,), (1,)), ((), ())), preferred_element_type=f32
    )

    @pl.when(step == pl.num_programs(0) - 1)
    def _():
        out_ref[...] = (
            total[:, :reps] + total[:, reps : 2 * reps] + total[:, 2 * reps : 3 * reps]
        )


def gram(rep_weights, covariate_codes):
    reps, people = rep_weights.shape
    variables = covariate_codes.shape[0]
    rows = pair_layout(variables)[2]
    block = 1024
    return pl.pallas_call(
        gram_kernel,
        grid=(people // block,),
        in_specs=[
            pl.BlockSpec((reps, block), lambda i: (0, i)),
            pl.BlockSpec((variables, block), lambda i: (0, i)),
        ],
        out_specs=pl.BlockSpec((rows, reps), lambda i: (0, 0)),
        out_shape=jax.ShapeDtypeStruct((rows, reps), f32),
        scratch_shapes=[pltpu.VMEM((rows, block), bf16), pltpu.VMEM((rows, 3 * reps), f32)],
        compiler_params=pltpu.CompilerParams(vmem_limit_bytes=vmem_bytes),
        cost_estimate=pl.CostEstimate(
            flops=6 * rows * reps * people, bytes_accessed=4 * reps * people, transcendentals=0
        ),
    )(rep_weights, covariate_codes)


def solve_kernel(variables, sums_ref, controls_ref, out_ref, mat, rhs, coef, sol):
    size, _, reps = mat.shape
    offsets, singles, _ = pair_layout(variables)
    kept = base_levels - first_kept
    starts = [0] + [base_levels + kept * (v - 1) for v in range(1, variables)]
    firsts = [0] + [first_kept] * (variables - 1)
    mat[...] = jnp.zeros_like(mat)
    for v in range(variables):
        first, count = firsts[v], base_levels - firsts[v]
        single = sums_ref[singles + v * base_levels + first : singles + (v + 1) * base_levels, :]
        rhs[starts[v] : starts[v] + count, :] = (
            controls_ref[starts[v] : starts[v] + count, :] - single
        )
        for c in range(count):
            mat[starts[v] + c, starts[v] + c : starts[v] + c + 1, :] = single[c : c + 1, :]
    for (u, v), row in offsets.items():
        for c in range(base_levels - firsts[u]):
            at = row + c * base_levels + first_kept
            mat[starts[u] + c, starts[v] : starts[v] + kept, :] = sums_ref[at : at + kept, :]

    for block in range(size // 8):
        low = block * 8

        def eliminate(inner, carry, low=low, block=block):
            k = low + inner
            row = mat[k, low:, :]
            pivot = mat[k, pl.ds(k, 1), :]
            place = lax.broadcasted_iota(jnp.int32, row.shape, 0) + low
            factor = jnp.where(place > k, row * (1.0 / pivot), 0.0)
            coef[low:, :] = factor
            rhs[low:, :] = rhs[low:, :] - factor * rhs[pl.ds(k, 1), :]
            for other in range(block, size // 8):
                part = row[other * 8 - low :, :]
                for i in range(other * 8, other * 8 + 8):
                    mat[i, other * 8 :, :] = mat[i, other * 8 :, :] - coef[i : i + 1, :] * part
            return carry

        lax.fori_loop(0, 8, eliminate, 0)

    sol[...] = jnp.zeros_like(sol)
    for block in reversed(range(size // 8)):
        low = block * 8

        def substitute(inner, carry, low=low):
            k = low + 7 - inner
            known = jnp.sum(mat[k, low:, :] * sol[low:, :], axis=0, keepdims=True)
            sol[pl.ds(k, 1), :] = (rhs[pl.ds(k, 1), :] - known) / mat[k, pl.ds(k, 1), :]
            return carry

        lax.fori_loop(0, 8, substitute, 0)

    out_ref[...] = jnp.zeros_like(out_ref)
    for v in range(variables):
        count = base_levels - firsts[v]
        at = v * base_levels + firsts[v]
        out_ref[at : at + count, :] = sol[starts[v] : starts[v] + count, :]


def solve(sums, controls, variables):
    reps = sums.shape[1]
    size = controls.shape[0]
    return pl.pallas_call(
        functools.partial(solve_kernel, variables),
        in_specs=[pl.BlockSpec(memory_space=pltpu.VMEM)] * 2,
        out_specs=pl.BlockSpec(memory_space=pltpu.VMEM),
        out_shape=jax.ShapeDtypeStruct((variables * base_levels, reps), f32),
        scratch_shapes=[
            pltpu.VMEM((size, size, reps), f32),
            pltpu.VMEM((size, reps), f32),
            pltpu.VMEM((size, reps), f32),
            pltpu.VMEM((size, reps), f32),
        ],
        compiler_params=pltpu.CompilerParams(vmem_limit_bytes=vmem_bytes),
    )(sums, jnp.broadcast_to(controls[:, None], (size, reps)))


def calibrate_kernel(x_ref, w_ref, codes_ref, cal_ref, sent_ref):
    variables = codes_ref.shape[0]
    design = jnp.concatenate(
        [one_hot(codes_ref[v : v + 1, :], base_levels) for v in range(variables)], axis=0
    )
    pieces = split3(x_ref[...], 0)
    adjustment = lax.dot_general(
        pieces,
        jnp.concatenate([design] * 3, axis=0),
        (((0,), (0,)), ((), ())),
        preferred_element_type=f32,
    )
    calibrated = w_ref[...] * (1.0 + adjustment)
    cal_ref[...] = calibrated
    sent_ref[...] = calibrated.astype(bf16)


def calibrate(x, rep_weights, covariate_codes):
    reps, people = rep_weights.shape
    variables = covariate_codes.shape[0]
    block = 1024
    return pl.pallas_call(
        calibrate_kernel,
        grid=(people // block,),
        in_specs=[
            pl.BlockSpec(x.shape, lambda i: (0, 0)),
            pl.BlockSpec((reps, block), lambda i: (0, i)),
            pl.BlockSpec((variables, block), lambda i: (0, i)),
        ],
        out_specs=[pl.BlockSpec((reps, block), lambda i: (0, i))] * 2,
        out_shape=[
            jax.ShapeDtypeStruct((reps, people), f32),
            jax.ShapeDtypeStruct((reps, people), bf16),
        ],
        compiler_params=pltpu.CompilerParams(vmem_limit_bytes=vmem_bytes),
    )(x, rep_weights, covariate_codes)


def table_kernel(tracts, sent_ref, about_ref, grid_ref, out_ref, masked):
    step = pl.program_id(0) * pl.num_programs(1) + pl.program_id(1)
    reps = sent_ref.shape[1]
    sent = sent_ref[0]
    income = about_ref[0, 0:1, :]
    tract = about_ref[0, 1:2, :]
    for k in range(tracts):
        inside = jnp.where(tract == float(k), 1.0, 0.0).astype(bf16)
        masked[k * reps : (k + 1) * reps, :] = sent * inside
    centers = (grid_ref[...].astype(f32) - grid_middle) * grid_step
    half = (centers - income) * (0.5 / smooth_width)
    smoothed = (0.5 + 0.5 * jnp.tanh(half)).astype(bf16)
    product = lax.dot_general(
        masked[...], smoothed, (((1,), (1,)), ((), ())), preferred_element_type=f32
    )

    @pl.when(step == 0)
    def _():
        out_ref[...] = product

    @pl.when(step > 0)
    def _():
        out_ref[...] += product


def partial_tables(sent, about, grid_column, tracts):
    sources, reps, people = sent.shape
    thresholds = grid_column.shape[0]
    block = 1024
    return pl.pallas_call(
        functools.partial(table_kernel, tracts),
        grid=(sources, people // block),
        in_specs=[
            pl.BlockSpec((1, reps, block), lambda s, i: (s, 0, i)),
            pl.BlockSpec((1, 2, block), lambda s, i: (s, 0, i)),
            pl.BlockSpec((thresholds, 1), lambda s, i: (0, 0)),
        ],
        out_specs=pl.BlockSpec((tracts * reps, thresholds), lambda s, i: (0, 0)),
        out_shape=jax.ShapeDtypeStruct((tracts * reps, thresholds), f32),
        scratch_shapes=[pltpu.VMEM((tracts * reps, block), bf16)],
        compiler_params=pltpu.CompilerParams(vmem_limit_bytes=vmem_bytes),
    )(sent, about, grid_column)


def shards(rep_weights, covariate_codes, tract_of, log_income, controls, threshold_grid):
    reps, people = rep_weights.shape
    variables = covariate_codes.shape[0]
    tracts = lax.axis_size("tract")
    recs = lax.axis_size("rec")
    share = threshold_grid.shape[0] // recs
    grid_column = lax.dynamic_slice_in_dim(
        threshold_grid, lax.axis_index("rec") * share, share, 0
    )[:, None]
    about = jnp.stack([log_income.astype(f32), tract_of[:, 0].astype(f32)])
    about = lax.all_gather(about, "rec")
    sums = lax.psum(gram(rep_weights, covariate_codes), ("rec", "tract"))
    x = solve(sums, controls, variables)
    calibrated, sent = calibrate(x, rep_weights, covariate_codes)
    sent = lax.all_gather(sent, "rec")
    tables = partial_tables(sent, about, grid_column, tracts)
    tables = lax.psum_scatter(tables, "tract", scatter_dimension=0, tiled=True)
    return calibrated, (tables / float(people * recs))[None]


def solution(mesh):
    placed = (
        P(None, ("rec", "tract")),
        P(None, ("rec", "tract")),
        P(("rec", "tract"), None),
        P(("rec", "tract")),
        P(),
        P(),
    )
    return jax.shard_map(
        shards,
        mesh=mesh,
        in_specs=placed,
        out_specs=(P(None, ("rec", "tract")), P("tract", None, "rec")),
        check_vma=False,
    )
```

```python
import functools

import jax
import jax.numpy as jnp
from jax import lax
from jax.experimental import pallas as pl
from jax.experimental.pallas import tpu as pltpu
from jax.sharding import PartitionSpec as P

smooth_width = 3.0 / 8192.0
grid_middle = 2048.0
grid_step = 3.0 / 2048.0
base_levels = 16
first_kept = 4
vmem_bytes = 48 * 1024 * 1024
bf16 = jnp.bfloat16
f32 = jnp.float32


def pair_layout(variables):
    offsets, row = {}, 0
    for u in range(variables):
        first = 0 if u == 0 else first_kept
        for v in range(u + 1, variables):
            offsets[u, v] = row
            row += (base_levels - first) * base_levels
    singles = row
    row += variables * base_levels
    return offsets, singles, row


def split3(value, axis):
    high = value.astype(bf16)
    rest = value - high.astype(f32)
    middle = rest.astype(bf16)
    low = (rest - middle.astype(f32)).astype(bf16)
    return jnp.concatenate([high, middle, low], axis=axis)


def one_hot(key, rows):
    width = key.shape[1]
    row = lax.broadcasted_iota(jnp.int32, (rows, width), 0)
    return jnp.where(row == key, 1.0, 0.0).astype(bf16)


def gram_kernel(w_ref, codes_ref, out_ref, pairs, total):
    step = pl.program_id(0)
    variables, _ = codes_ref.shape
    reps = w_ref.shape[0]
    offsets, singles, rows = pair_layout(variables)

    @pl.when(step == 0)
    def _():
        total[...] = jnp.zeros_like(total)
        pairs[rows:, :] = jnp.zeros((pairs.shape[0] - rows, pairs.shape[1]), bf16)

    pieces = split3(w_ref[...], 0)
    for (u, v), row in offsets.items():
        first = 0 if u == 0 else first_kept
        key = (codes_ref[u : u + 1, :] - first) * base_levels + codes_ref[v : v + 1, :]
        count = (base_levels - first) * base_levels
        pairs[row : row + count, :] = one_hot(key, count)
    for v in range(variables):
        row = singles + v * base_levels
        pairs[row : row + base_levels, :] = one_hot(codes_ref[v : v + 1, :], base_levels)
    total[...] += lax.dot_general(
        pairs[...], pieces, (((1,), (1,)), ((), ())), preferred_element_type=f32
    )

    @pl.when(step == pl.num_programs(0) - 1)
    def _():
        out_ref[...] = (
            total[:, :reps] + total[:, reps : 2 * reps] + total[:, 2 * reps : 3 * reps]
        )


def gram(rep_weights, covariate_codes, multiple):
    reps, people = rep_weights.shape
    variables = covariate_codes.shape[0]
    rows = -(-pair_layout(variables)[2] // multiple) * multiple
    block = 1024
    return pl.pallas_call(
        gram_kernel,
        grid=(people // block,),
        in_specs=[
            pl.BlockSpec((reps, block), lambda i: (0, i)),
            pl.BlockSpec((variables, block), lambda i: (0, i)),
        ],
        out_specs=pl.BlockSpec((rows, reps), lambda i: (0, 0)),
        out_shape=jax.ShapeDtypeStruct((rows, reps), f32),
        scratch_shapes=[pltpu.VMEM((rows, block), bf16), pltpu.VMEM((rows, 3 * reps), f32)],
        compiler_params=pltpu.CompilerParams(vmem_limit_bytes=vmem_bytes),
        cost_estimate=pl.CostEstimate(
            flops=6 * rows * reps * people, bytes_accessed=4 * reps * people, transcendentals=0
        ),
    )(rep_weights, covariate_codes)


def solve_kernel(variables, sums_ref, controls_ref, out_ref, mat, rhs, coef, sol):
    size, _, reps = mat.shape
    offsets, singles, _ = pair_layout(variables)
    kept = base_levels - first_kept
    starts = [0] + [base_levels + kept * (v - 1) for v in range(1, variables)]
    firsts = [0] + [first_kept] * (variables - 1)
    mat[...] = jnp.zeros_like(mat)
    for v in range(variables):
        first, count = firsts[v], base_levels - firsts[v]
        single = sums_ref[singles + v * base_levels + first : singles + (v + 1) * base_levels, :]
        rhs[starts[v] : starts[v] + count, :] = (
            controls_ref[starts[v] : starts[v] + count, :] - single
        )
        for c in range(count):
            mat[starts[v] + c, starts[v] + c : starts[v] + c + 1, :] = single[c : c + 1, :]
    for (u, v), row in offsets.items():
        for c in range(base_levels - firsts[u]):
            at = row + c * base_levels + first_kept
            mat[starts[u] + c, starts[v] : starts[v] + kept, :] = sums_ref[at : at + kept, :]

    for block in range(size // 8):
        low = block * 8

        def eliminate(inner, carry, low=low, block=block):
            k = low + inner
            row = mat[k, low:, :]
            pivot = mat[k, pl.ds(k, 1), :]
            place = lax.broadcasted_iota(jnp.int32, row.shape, 0) + low
            factor = jnp.where(place > k, row * (1.0 / pivot), 0.0)
            coef[low:, :] = factor
            rhs[low:, :] = rhs[low:, :] - factor * rhs[pl.ds(k, 1), :]
            for other in range(block, size // 8):
                part = row[other * 8 - low :, :]
                for i in range(other * 8, other * 8 + 8):
                    mat[i, other * 8 :, :] = mat[i, other * 8 :, :] - coef[i : i + 1, :] * part
            return carry

        lax.fori_loop(0, 8, eliminate, 0)

    sol[...] = jnp.zeros_like(sol)
    for block in reversed(range(size // 8)):
        low = block * 8

        def substitute(inner, carry, low=low):
            k = low + 7 - inner
            known = jnp.sum(mat[k, low:, :] * sol[low:, :], axis=0, keepdims=True)
            sol[pl.ds(k, 1), :] = (rhs[pl.ds(k, 1), :] - known) / mat[k, pl.ds(k, 1), :]
            return carry

        lax.fori_loop(0, 8, substitute, 0)

    out_ref[...] = jnp.zeros_like(out_ref)
    for v in range(variables):
        count = base_levels - firsts[v]
        at = v * base_levels + firsts[v]
        out_ref[at : at + count, :] = sol[starts[v] : starts[v] + count, :]


def solve(sums, controls, variables):
    reps = sums.shape[1]
    size = controls.shape[0]
    return pl.pallas_call(
        functools.partial(solve_kernel, variables),
        in_specs=[pl.BlockSpec(memory_space=pltpu.VMEM)] * 2,
        out_specs=pl.BlockSpec(memory_space=pltpu.VMEM),
        out_shape=jax.ShapeDtypeStruct((variables * base_levels, reps), f32),
        scratch_shapes=[
            pltpu.VMEM((size, size, reps), f32),
            pltpu.VMEM((size, reps), f32),
            pltpu.VMEM((size, reps), f32),
            pltpu.VMEM((size, reps), f32),
        ],
        compiler_params=pltpu.CompilerParams(vmem_limit_bytes=vmem_bytes),
    )(sums, jnp.broadcast_to(controls[:, None], (size, reps)))


def calibrate_kernel(x_ref, w_ref, codes_ref, cal_ref, sent_ref):
    variables = codes_ref.shape[0]
    design = jnp.concatenate(
        [one_hot(codes_ref[v : v + 1, :], base_levels) for v in range(variables)], axis=0
    )
    pieces = split3(x_ref[...], 0)
    adjustment = lax.dot_general(
        pieces,
        jnp.concatenate([design] * 3, axis=0),
        (((0,), (0,)), ((), ())),
        preferred_element_type=f32,
    )
    calibrated = w_ref[...] * (1.0 + adjustment)
    cal_ref[...] = calibrated
    sent_ref[...] = calibrated.astype(bf16)


def calibrate(x, rep_weights, covariate_codes):
    reps, people = rep_weights.shape
    variables = covariate_codes.shape[0]
    block = 1024
    return pl.pallas_call(
        calibrate_kernel,
        grid=(people // block,),
        in_specs=[
            pl.BlockSpec(x.shape, lambda i: (0, 0)),
            pl.BlockSpec((reps, block), lambda i: (0, i)),
            pl.BlockSpec((variables, block), lambda i: (0, i)),
        ],
        out_specs=[pl.BlockSpec((reps, block), lambda i: (0, i))] * 2,
        out_shape=[
            jax.ShapeDtypeStruct((reps, people), f32),
            jax.ShapeDtypeStruct((reps, people), bf16),
        ],
        compiler_params=pltpu.CompilerParams(vmem_limit_bytes=vmem_bytes),
    )(x, rep_weights, covariate_codes)


def table_kernel(tracts, sent_ref, about_ref, grid_ref, out_ref, masked):
    step = pl.program_id(0) * pl.num_programs(1) + pl.program_id(1)
    reps = sent_ref.shape[1]
    sent = sent_ref[0]
    income = about_ref[0, 0:1, :]
    tract = about_ref[0, 1:2, :]
    for k in range(tracts):
        inside = jnp.where(tract == float(k), 1.0, 0.0).astype(bf16)
        masked[k * reps : (k + 1) * reps, :] = sent * inside
    centers = (grid_ref[...].astype(f32) - grid_middle) * grid_step
    half = (centers - income) * (0.5 / smooth_width)
    smoothed = (0.5 + 0.5 * jnp.tanh(half)).astype(bf16)
    product = lax.dot_general(
        masked[...], smoothed, (((1,), (1,)), ((), ())), preferred_element_type=f32
    )

    @pl.when(step == 0)
    def _():
        out_ref[...] = product

    @pl.when(step > 0)
    def _():
        out_ref[...] += product


def partial_tables(sent, about, grid_column, tracts):
    sources, reps, people = sent.shape
    thresholds = grid_column.shape[0]
    block = 1024
    return pl.pallas_call(
        functools.partial(table_kernel, tracts),
        grid=(sources, people // block),
        in_specs=[
            pl.BlockSpec((1, reps, block), lambda s, i: (s, 0, i)),
            pl.BlockSpec((1, 2, block), lambda s, i: (s, 0, i)),
            pl.BlockSpec((thresholds, 1), lambda s, i: (0, 0)),
        ],
        out_specs=pl.BlockSpec((tracts * reps, thresholds), lambda s, i: (0, 0)),
        out_shape=jax.ShapeDtypeStruct((tracts * reps, thresholds), f32),
        scratch_shapes=[pltpu.VMEM((tracts * reps, block), bf16)],
        compiler_params=pltpu.CompilerParams(vmem_limit_bytes=vmem_bytes),
    )(sent, about, grid_column)


def greet(axes):
    barrier = pltpu.get_barrier_semaphore()
    count = 0
    for name, size in axes:
        me = lax.axis_index(name)
        for d in range(1, size):
            pl.semaphore_signal(
                barrier,
                inc=1,
                device_id={name: lax.rem(me + d, size)},
                device_id_type=pl.DeviceIdType.MESH,
            )
            count += 1
    pl.semaphore_wait(barrier, count)


def send(source, target, sems, slot, name, peer):
    copy = pltpu.make_async_remote_copy(
        src_ref=source,
        dst_ref=target,
        send_sem=sems.at[0, slot],
        recv_sem=sems.at[1, slot],
        device_id={name: peer},
        device_id_type=pl.DeviceIdType.MESH,
    )
    copy.start()
    return copy


def total_kernel(
    recs, tracts, x_ref, about_ref, out_ref, around_ref, from_rec, part, from_tract,
    about_sems, rec_sems, tract_sems, tract_back, rec_back,
):
    rec, tract = lax.axis_index("rec"), lax.axis_index("tract")
    large, small = part.shape[0], from_tract.shape[1]
    greet([("rec", recs), ("tract", tracts)])

    arriving = []
    for d in range(1, recs):
        peer = lax.rem(rec + d, recs)
        rows = pl.ds(pl.multiple_of(peer * large, 8), large)
        arriving.append(send(x_ref.at[rows], from_rec.at[d], rec_sems, d, "rec", peer))
    about = []
    for d in range(1, recs):
        peer = lax.rem(rec + d, recs)
        about.append(send(about_ref, around_ref.at[rec], about_sems, d, "rec", peer))
    around_ref[rec] = about_ref[...]
    for copy in arriving:
        copy.wait()
    value = x_ref[pl.ds(pl.multiple_of(rec * large, 8), large), :]
    for d in range(1, recs):
        value = value + from_rec[d]
    part[...] = value

    arriving = []
    for d in range(1, tracts):
        peer = lax.rem(tract + d, tracts)
        rows = pl.ds(pl.multiple_of(peer * small, 8), small)
        arriving.append(send(part.at[rows], from_tract.at[d], tract_sems, d, "tract", peer))
    for copy in arriving:
        copy.wait()
    value = part[pl.ds(pl.multiple_of(tract * small, 8), small), :]
    for d in range(1, tracts):
        value = value + from_tract[d]
    mine = pl.ds(pl.multiple_of(rec * large + tract * small, 8), small)
    out_ref[mine, :] = value

    arriving = []
    for d in range(1, tracts):
        peer = lax.rem(tract + d, tracts)
        arriving.append(send(out_ref.at[mine], out_ref.at[mine], tract_back, d, "tract", peer))
    for copy in arriving:
        copy.wait()
    mine = pl.ds(pl.multiple_of(rec * large, 8), large)
    arriving = []
    for d in range(1, recs):
        peer = lax.rem(rec + d, recs)
        arriving.append(send(out_ref.at[mine], out_ref.at[mine], rec_back, d, "rec", peer))
    for copy in arriving + about:
        copy.wait()


def totals(x, about, recs, tracts):
    rows, reps = x.shape
    large, small = rows // recs, rows // (recs * tracts)
    dma = pltpu.SemaphoreType.DMA
    return pl.pallas_call(
        functools.partial(total_kernel, recs, tracts),
        in_specs=[pl.BlockSpec(memory_space=pltpu.VMEM)] * 2,
        out_specs=[pl.BlockSpec(memory_space=pltpu.VMEM)] * 2,
        out_shape=[
            jax.ShapeDtypeStruct((rows, reps), f32),
            jax.ShapeDtypeStruct((recs,) + about.shape, f32),
        ],
        scratch_shapes=[
            pltpu.VMEM((recs, large, reps), f32),
            pltpu.VMEM((large, reps), f32),
            pltpu.VMEM((tracts, small, reps), f32),
            dma((2, recs)),
            dma((2, recs)),
            dma((2, tracts)),
            dma((2, tracts)),
            dma((2, recs)),
        ],
        compiler_params=pltpu.CompilerParams(
            vmem_limit_bytes=vmem_bytes, collective_id=0, has_side_effects=True
        ),
    )(x, about)


def scatter_kernel(tracts, scale, x_ref, out_ref, landed, sems):
    tract = lax.axis_index("tract")
    reps = out_ref.shape[1]
    greet([("tract", tracts)])
    arriving = []
    for d in range(1, tracts):
        peer = lax.rem(tract + d, tracts)
        rows = pl.ds(pl.multiple_of(peer * reps, 8), reps)
        arriving.append(send(x_ref.at[rows], landed.at[d], sems, d, "tract", peer))
    value = x_ref[pl.ds(pl.multiple_of(tract * reps, 8), reps), :]
    for d in range(1, tracts):
        arriving[d - 1].wait()
        value = value + landed[d]
    out_ref[0] = value / scale


def scatter(x, reps, tracts, scale):
    columns = x.shape[1]
    return pl.pallas_call(
        functools.partial(scatter_kernel, tracts, scale),
        in_specs=[pl.BlockSpec(memory_space=pltpu.VMEM)],
        out_specs=pl.BlockSpec(memory_space=pltpu.VMEM),
        out_shape=jax.ShapeDtypeStruct((1, reps, columns), f32),
        scratch_shapes=[
            pltpu.VMEM((tracts, reps, columns), f32),
            pltpu.SemaphoreType.DMA((2, tracts)),
        ],
        compiler_params=pltpu.CompilerParams(
            vmem_limit_bytes=vmem_bytes, collective_id=1, has_side_effects=True
        ),
    )(x)


def shards(rep_weights, covariate_codes, tract_of, log_income, controls, threshold_grid):
    reps, people = rep_weights.shape
    variables = covariate_codes.shape[0]
    tracts = lax.axis_size("tract")
    recs = lax.axis_size("rec")
    share = threshold_grid.shape[0] // recs
    grid_column = lax.dynamic_slice_in_dim(
        threshold_grid, lax.axis_index("rec") * share, share, 0
    )[:, None]
    about = jnp.stack([log_income.astype(f32), tract_of[:, 0].astype(f32)])
    sums = gram(rep_weights, covariate_codes, 8 * recs * tracts)
    sums, about = totals(sums, about, recs, tracts)
    x = solve(sums, controls, variables)
    calibrated, sent = calibrate(x, rep_weights, covariate_codes)
    sent = lax.all_gather(sent, "rec")
    tables = partial_tables(sent, about, grid_column, tracts)
    return calibrated, scatter(tables, reps, tracts, float(people * recs))


def solution(mesh):
    placed = (
        P(None, ("rec", "tract")),
        P(None, ("rec", "tract")),
        P(("rec", "tract"), None),
        P(("rec", "tract")),
        P(),
        P(),
    )
    return jax.shard_map(
        shards,
        mesh=mesh,
        in_specs=placed,
        out_specs=(P(None, ("rec", "tract")), P("tract", None, "rec")),
        check_vma=False,
    )
```
